32 devices in a mesh: member: 8 (over y, x, core), sub: 4 (over z).
Axes of the slice: x: 2, y: 2, z: 4, core: 2. Of those that a mesh axis runs over, the one named last changes fastest.
Arguments:
- velocity: float32 [8, 3, 64, 32, 128], P('member', None, 'sub'), may hold values from -8 to 8
- forcing: float32 [8, 3, 64, 32, 128], P('member', None, 'sub'), may hold values from -16 to 16
Outputs:
- new_velocity: float32 [8, 3, 64, 32, 128], P('member', None, 'sub')
The draws below stay inside these ranges and needn't reach their ends.
All inputs are finite; a program needn't handle non-finite values.
Results may differ from the reference program's by a relative error of at most 0.00029.
Values sent between devices are 32-bit elements; how exact they have to be, the bound alone decides.
No kernel may reach another device: no remote copies, remote signals or barrier semaphores. Data moves between devices by JAX's collectives and lax.ppermute only.
A program may use at most 64 MiB of HBM per device.

```python
import math
import jax
import jax.numpy as jnp
from jax import lax

NY = 32
NZ = 128
SWEEPS = 8
MEMBERS = 8
NX = 64


def draw_velocity(key, part):
    layer_key, noise_key = jax.random.split(key, 2)
    full_shape = (MEMBERS, 3, NX, NY, NZ)
    layer_scale = jnp.exp(jax.random.uniform(layer_key, (NX,), jnp.float32, math.log(1.5), math.log(5.0)))
    noise_draw = jax.random.normal(noise_key, full_shape, jnp.float32)
    values = noise_draw * layer_scale[None, None, :, None, None]
    return jnp.clip(values, -8.0, 8.0)


def draw_forcing(key, part):
    rough_key, amp_key, phase_key, sign_key = jax.random.split(key, 4)
    full_shape = (MEMBERS, 3, NX, NY, NZ)
    rough_part = jnp.clip(2.0 * jax.random.normal(rough_key, full_shape, jnp.float32), -8.0, 8.0)
    amplitude = jnp.exp(jax.random.uniform(amp_key, (MEMBERS, 3), jnp.float32, math.log(2.0), math.log(4.0)))
    phases = jax.random.uniform(phase_key, (MEMBERS, 3, 2), jnp.float32, -math.pi, math.pi)
    signs = jnp.where(jax.random.bernoulli(sign_key, 0.5, (MEMBERS, 3)), 1.0, -1.0).astype(jnp.float32)
    along_x = 2.0 * math.pi * jnp.arange(NX).astype(jnp.float32) / NX
    along_y = 2.0 * math.pi * jnp.arange(NY).astype(jnp.float32) / NY
    profile_x = 1.0 + 0.6 * jnp.cos(along_x[None, None, :] + phases[:, :, 0:1])
    profile_y = 1.0 + 0.25 * jnp.cos(along_y[None, None, :] + phases[:, :, 1:2])
    smooth_part = (signs * amplitude)[:, :, None, None, None] * profile_x[:, :, :, None, None] * profile_y[:, :, None, :, None]
    return jnp.clip(rough_part + smooth_part, -16.0, 16.0)


def setup_inputs(seed: int = 0) -> dict:
    seeds = jax.random.split(jax.random.key(seed), 3)
    velocity = draw_velocity(jax.random.fold_in(seeds[2], 71), 0)
    forcing = draw_forcing(jax.random.fold_in(seeds[2], 71), 0)
    return dict(velocity=velocity, forcing=forcing)


TIME_STEP = 0.25
EDDY_COEFF = 1.0
BASE_VISCOSITY = 1.0
LOWER_EDGE = 0.1
UPPER_EDGE = 1.9


def step_sizes(sweep_count):
    middle = (UPPER_EDGE + LOWER_EDGE) / 2
    radius = (UPPER_EDGE - LOWER_EDGE) / 2
    return [1.0 / (middle + radius * math.cos(math.pi * (2 * position + 1) / (2 * sweep_count))) for position in range(sweep_count)]


def reference(velocity, forcing):
    members = velocity.shape[0]
    mean_flow = jnp.sum(velocity, 0) / members
    spread = jnp.sum(jnp.sum((velocity - mean_flow) ** 2, 1), 0) / members
    viscosity = BASE_VISCOSITY + EDDY_COEFF * TIME_STEP * spread
    faces = []
    for grid_axis in range(3):
        faces.append(0.5 * (viscosity + jnp.roll(viscosity, -1, grid_axis)))
        faces.append(0.5 * (viscosity + jnp.roll(viscosity, 1, grid_axis)))
    diagonal = 1.0 + TIME_STEP * (faces[0] + faces[1] + faces[2] + faces[3] + faces[4] + faces[5])
    sizes_list = step_sizes(SWEEPS)

    def operator(field):
        neighbours = faces[0] * jnp.roll(field, -1, 1) + faces[1] * jnp.roll(field, 1, 1)
        neighbours = neighbours + faces[2] * jnp.roll(field, -1, 2) + faces[3] * jnp.roll(field, 1, 2)
        neighbours = neighbours + faces[4] * jnp.roll(field, -1, 3) + faces[5] * jnp.roll(field, 1, 3)
        return diagonal * field - TIME_STEP * neighbours

    def advance(member_pair):
        member_velocity, member_forcing = member_pair
        terms = [mean_flow[grid_axis] * ((jnp.roll(member_velocity, -1, grid_axis + 1) - jnp.roll(member_velocity, 1, grid_axis + 1)) * 0.5) for grid_axis in range(3)]
        transport = terms[0] + terms[1] + terms[2]
        source = member_velocity - TIME_STEP * transport + TIME_STEP * member_forcing
        field = source
        for step_size in sizes_list:
            field = field + step_size * (source - operator(field)) / diagonal
        return field

    return lax.map(advance, (velocity, forcing))
```

```python
import functools
import math

import jax
import jax.numpy as jnp
from jax import lax
from jax.experimental import pallas as pl
from jax.experimental.pallas import tpu as pltpu
from jax.sharding import PartitionSpec as P

SWEEPS = 8


TIME_STEP = 0.25
EDDY_COEFF = 1.0
BASE_VISCOSITY = 1.0
LOWER_EDGE = 0.1
UPPER_EDGE = 1.9

ROWS = 8
PIECES = ((0, 4), (4, 8))
EARLY = 4
VMEM_LIMIT = 40 * 1024 * 1024


def step_sizes(sweep_count):
    middle = (UPPER_EDGE + LOWER_EDGE) / 2
    radius = (UPPER_EDGE - LOWER_EDGE) / 2
    return [
        1.0 / (middle + radius * math.cos(math.pi * (2 * position + 1) / (2 * sweep_count)))
        for position in range(sweep_count)
    ]


def north(planes):
    return planes[1:] + [pltpu.roll(planes[0], ROWS - 1, 0)]


def south(planes):
    return [pltpu.roll(planes[-1], 1, 0)] + planes[:-1]


def upper(plane):
    return pltpu.roll(plane, plane.shape[-1] - 1, 1)


def lower(plane):
    return pltpu.roll(plane, 1, 1)


def rows_of(j, count):
    return pl.ds(j, ROWS, stride=count)


def parity():
    return lax.rem(lax.axis_index("member"), 2)


def for_layers(count, body, unroll=1):
    def step(i, carry):
        body(i)
        return carry

    lax.fori_loop(0, count, step, 0, unroll=unroll)


def arrange_kernel(vel, force, vp, gp, first, last):
    comps, nx, planes = vp.shape[:3]

    def body(x):
        for c in range(comps):
            for j in range(planes):
                value = vel[0, c, x, rows_of(j, planes), :]
                vp[c, x, j] = value
                gp[c, x, j] = value + TIME_STEP * force[0, c, x, rows_of(j, planes), :]

    for_layers(nx, body, 2)
    first[...] = vp[:, :1]
    last[...] = vp[:, nx - 1 :]


def sums_kernel(pieces, vp, other, *outs):
    comps, nx, planes = vp.shape[:3]
    side = parity()
    for (near, far), out in zip(pieces, outs):
        start = jnp.where(side == 0, near, nx - far)

        def body(i, out=out, start=start):
            x = start + i
            for j in range(planes):
                squares = None
                for c in range(comps):
                    a = vp[c, x, j]
                    b = other[0, c, x, rows_of(j, planes), :]
                    out[c, i, j] = a + b
                    both = a * a + b * b
                    squares = both if squares is None else squares + both
                out[comps, i, j] = squares

        for_layers(far - near, body)


def stats_kernel(members, add_two, *refs):
    out = refs[-1]
    comps, layers, planes = out.shape[0] - 1, out.shape[1], out.shape[2]

    def body(i):
        for j in range(planes):
            def total(c):
                value = refs[0][c, i, j]
                return value + refs[1][c, i, j] if add_two else value

            spread = total(comps) * (1.0 / members)
            for c in range(comps):
                mean = total(c) * (1.0 / members)
                out[c, i, j] = mean
                spread = spread - mean * mean
            out[comps, i, j] = BASE_VISCOSITY + EDDY_COEFF * TIME_STEP * spread

    for_layers(layers, body)


def source_kernel(piece, vp, gp, below, above, mine, theirs, out_mine, out_theirs):
    comps, nx, planes = vp.shape[:3]
    near, far = piece
    side = parity()
    for which, stats, out in ((side, mine, out_mine), (1 - side, theirs, out_theirs)):
        start = jnp.where(which == 0, near, nx - far)

        def body(i, stats=stats, out=out, start=start):
            x = start + i
            down, up = jnp.maximum(x - 1, 0), jnp.minimum(x + 1, nx - 1)
            for c in range(comps):
                here = [vp[c, x, j] for j in range(planes)]
                ns, ss = north(here), south(here)
                for j in range(planes):
                    west = jnp.where(x == 0, below[c, 0, j], vp[c, down, j])
                    east = jnp.where(x == nx - 1, above[c, 0, j], vp[c, up, j])
                    transport = (
                        stats[0, i, j] * (east - west)
                        + stats[1, i, j] * (ns[j] - ss[j])
                        + stats[2, i, j] * (upper(here[j]) - lower(here[j]))
                    )
                    out[c, i, j] = gp[c, x, j] - (0.5 * TIME_STEP) * transport

        for_layers(far - near, body)


def relax(load_center, load_out, load_in, coef, load_source, store, comps, planes, step_size, flip):
    near_coef, far_coef = (0, 1) if not flip else (1, 0)
    for c in range(comps):
        here = [load_center(c, j) for j in range(planes)]
        ns, ss = north(here), south(here)
        for j in range(planes):
            image = load_source(c, j)
            image = image + coef(near_coef, j) * load_in(c, j)
            image = image + coef(far_coef, j) * load_out(c, j)
            image = image + coef(2, j) * ns[j] + coef(3, j) * ss[j]
            image = image + coef(4, j) * upper(here[j]) + coef(5, j) * lower(here[j])
            store(c, j, (1.0 - step_size) * here[j] + step_size * image)


def early_kernel(pieces, early, sizes, count, *refs):
    number = len(pieces)
    n_early = sum(1 for piece in pieces if piece[1] <= early)
    refs = list(refs)

    def take(n):
        head = refs[:n]
        del refs[:n]
        return head

    src_mine, src_theirs = take(number), take(number)
    stat_mine, stat_theirs = take(number), take(number)
    visc_got, visc_other = take(1)[0], take(1)[0]
    halo_mine, halo_theirs = take(n_early), take(n_early)
    coef, scaled, edges, middle = take(4)
    visc, field = take(2)
    depth = len(sizes)
    comps, planes = scaled.shape[0], scaled.shape[2]
    side = parity()

    for which, stats, srcs in ((side, stat_mine, src_mine), (1 - side, stat_theirs, src_theirs)):
        for (near, far), stat, src in zip(pieces, stats, srcs):
            start = jnp.where(which == 0, near, count - far)
            visc[pl.ds(depth + start, far - near)] = stat[comps]
            for c in range(comps):
                field[0, c, pl.ds(early + start, far - near)] = src[c]
    for which, got in ((side, visc_got), (1 - side, visc_other)):
        for near, far in pieces:
            start = jnp.where(which == 0, depth + count + near, depth - far)
            visc[pl.ds(start, far - near)] = got[near:far]
    for which, halos in ((side, halo_mine), (1 - side, halo_theirs)):
        for (near, far), halo in zip(pieces, halos):
            start = jnp.where(which == 0, early + count + near, early - far)
            for c in range(comps):
                field[0, c, pl.ds(start, far - near)] = halo[c]

    half = 0.5 * TIME_STEP

    def coefs(i):
        x = i + 1
        here = [visc[x, j] for j in range(planes)]
        ns, ss = north(here), south(here)
        for j in range(planes):
            faces = [
                here[j] + visc[x + 1, j],
                here[j] + visc[x - 1, j],
                here[j] + ns[j],
                here[j] + ss[j],
                here[j] + upper(here[j]),
                here[j] + lower(here[j]),
            ]
            total = (faces[0] + faces[1]) + (faces[2] + faces[3]) + (faces[4] + faces[5])
            inverse = 1.0 / (1.0 + half * total)
            scale = half * inverse
            for a in range(6):
                coef[a, x, j] = faces[a] * scale
            coef[6, x, j] = inverse

    for_layers(count + 2 * depth - 2, coefs)

    def scale_source(i):
        x = i + depth - early
        for c in range(comps):
            for j in range(planes):
                scaled[c, x, j] = field[0, c, i, j] * coef[6, x, j]

    for_layers(count + 2 * early, scale_source)

    total = count + 2 * early
    for k in range(depth + 1):
        if k:
            now, before = field.at[k], field.at[k - 1]

            def body(i, k=k, now=now, before=before):
                p = k + i
                x = p + depth - early

                def store(c, j, value):
                    if k < depth:
                        now[c, p, j] = value
                    else:
                        middle[c, i, rows_of(j, planes), :] = value

                relax(
                    lambda c, j: before[c, p, j],
                    lambda c, j: before[c, p - 1, j],
                    lambda c, j: before[c, p + 1, j],
                    lambda a, j: coef[a, x, j],
                    lambda c, j: scaled[c, x, j],
                    store,
                    comps,
                    planes,
                    sizes[k - 1],
                    False,
                )

            for_layers(total - 2 * k, body, 2)
        if k < depth:
            for c in range(comps):
                edges[k, 0, c, 0] = field[k, c, k]
                edges[k, 0, c, 1] = field[k, c, k + 1]
                edges[k, 1, c, 0] = field[k, c, total - 1 - k]
                edges[k, 1, c, 1] = field[k, c, total - 2 - k]


def late_kernel(pieces, early, sizes, count, *refs):
    n_late = sum(1 for piece in pieces if piece[1] > early)
    late = [piece for piece in pieces if piece[1] > early]
    refs = list(refs)

    def take(n):
        head = refs[:n]
        del refs[:n]
        return head

    coef, scaled, edges, middle = take(4)
    halo_mine, halo_theirs = take(n_late), take(n_late)
    out = take(1)[0]
    field, source, tail, sems = take(4)
    depth = len(sizes)
    width = depth - early
    comps, planes = scaled.shape[0], scaled.shape[2]
    side = parity()
    total = count + 2 * depth

    mid = pltpu.make_async_copy(middle, out.at[0, :, width : count - width], sems.at[0])
    mid.start()

    for which, halos in ((side, halo_mine), (1 - side, halo_theirs)):
        high = which == 0
        slot = 1 - which
        for (near, far), halo in zip(late, halos):
            for i in range(far - near):
                position = jnp.where(high, depth - 1 - near - i, depth - far + i)
                x = jnp.where(high, depth + count + near + i, depth - far + i)
                for c in range(comps):
                    for j in range(planes):
                        value = halo[c, i, j]
                        field[0, slot, c, position, j] = value
                        source[slot, c, position, j] = value * coef[6, x, j]
    for i in range(width, 2 * depth - early):
        for c in range(comps):
            source[0, c, i] = scaled[c, i]
            source[1, c, i] = scaled[c, total - 1 - i]
    for s in range(2):
        for c in range(comps):
            for e in range(2):
                field[0, s, c, width + e] = edges[0, s, c, e]

    def sweep(k, carry):
        step_size = jnp.float32(sizes[0])
        for position in range(1, depth):
            step_size = jnp.where(k == position + 1, jnp.float32(sizes[position]), step_size)
        for s in range(2):
            for r in range(width):
                inner = k + r
                x = inner if s == 0 else total - 1 - inner

                def store(c, j, value, s=s, r=r):
                    field[k, s, c, r, j] = value

                relax(
                    lambda c, j: field[k - 1, s, c, r + 1, j],
                    lambda c, j: field[k - 1, s, c, r, j],
                    lambda c, j: field[k - 1, s, c, r + 2, j],
                    lambda a, j: coef[a, x, j],
                    lambda c, j: source[s, c, inner, j],
                    store,
                    comps,
                    planes,
                    step_size,
                    s == 1,
                )
        edge = jnp.minimum(k, depth - 1)
        for s in range(2):
            for c in range(comps):
                for e in range(2):
                    field[k, s, c, width + e] = edges[edge, s, c, e]
        return carry

    lax.fori_loop(1, depth + 1, sweep, 0)
    copies = []
    for s in range(2):
        for r in range(width):
            place = r if s == 0 else width - 1 - r
            for c in range(comps):
                for j in range(planes):
                    tail[s, c, place, rows_of(j, planes), :] = field[depth, s, c, r, j]
        where = 0 if s == 0 else count - width
        copy = pltpu.make_async_copy(
            tail.at[s], out.at[0, :, where : where + width], sems.at[1 + s]
        )
        copy.start()
        copies.append(copy)
    for copy in copies:
        copy.wait()
    mid.wait()


def vmem(n):
    return [pl.BlockSpec(memory_space=pltpu.VMEM)] * n


def call(kernel, outs, ins, flops, scratch=(), any_out=False, name=None):
    shapes = [jax.ShapeDtypeStruct(shape, jnp.float32) for shape in outs]
    size = 4 * sum(math.prod(shape) for shape in outs) + 4 * sum(x.size for x in ins)
    result = pl.pallas_call(
        kernel,
        out_shape=shapes,
        in_specs=vmem(len(ins)),
        out_specs=[pl.BlockSpec(memory_space=pl.ANY)] * len(outs) if any_out else vmem(len(outs)),
        scratch_shapes=list(scratch),
        compiler_params=pltpu.CompilerParams(vmem_limit_bytes=VMEM_LIMIT),
        cost_estimate=pl.CostEstimate(flops=flops, bytes_accessed=size, transcendentals=0),
        name=name,
    )(*ins)
    return result


def fast(velocity, forcing):
    members = lax.axis_size("member")
    subs = lax.axis_size("sub")
    _, comps, nx, ny, nz = velocity.shape
    planes = ny // ROWS
    layer = (planes, ROWS, nz)
    sizes = step_sizes(SWEEPS)
    depth = SWEEPS
    bits = members.bit_length() - 1
    f32 = jnp.float32

    swap = [(m, m ^ 1) for m in range(members)]

    def pair(step):
        order = [list(range(1, bits)), list(range(2, bits)) + [1]]
        return [(m, m ^ (1 << order[m % 2][step])) for m in range(members)]

    def along(mine):
        moves = []
        for m in range(members):
            step = -1 if (m % 2 == 0) == mine else 1
            for s in range(subs):
                moves.append((m * subs + s, m * subs + (s + step) % subs))
        return moves

    other = lax.ppermute(velocity, "member", swap)
    vp, gp, first, last = call(
        arrange_kernel,
        [(comps, nx, *layer)] * 2 + [(comps, 1, *layer)] * 2,
        [velocity, forcing],
        10 * velocity.size,
        name="arrange",
    )
    above = lax.ppermute(first, "sub", [(s, (s - 1) % subs) for s in range(subs)])
    below = lax.ppermute(last, "sub", [(s, (s + 1) % subs) for s in range(subs)])
    sums = call(
        functools.partial(sums_kernel, PIECES),
        [(comps + 1, far - near, *layer) for near, far in PIECES],
        [vp, other],
        6 * velocity.size,
        name="sums",
    )
    stats_mine, stats_theirs, src_mine, src_theirs, halo_mine, halo_theirs = [], [], [], [], [], []
    for (near, far), part in zip(PIECES, sums):
        terms = [part]
        for step in range(bits - 1):
            part = terms[0] + terms[1] if len(terms) == 2 else terms[0]
            terms = [part, lax.ppermute(part, "member", pair(step))]
        stats = call(
            functools.partial(stats_kernel, members, len(terms) == 2),
            [(comps + 1, far - near, *layer)],
            terms,
            10 * part.size,
            name="stats",
        )[0]
        stats_mine.append(stats)
        stats_theirs.append(lax.ppermute(stats, "member", swap))
        mine, theirs = call(
            functools.partial(source_kernel, (near, far)),
            [(comps, far - near, *layer)] * 2,
            [vp, gp, below, above, stats, stats_theirs[-1]],
            20 * part.size,
            name="source",
        )
        src_mine.append(mine)
        src_theirs.append(theirs)
        halo_mine.append(lax.ppermute(mine, ("member", "sub"), along(True)))
        halo_theirs.append(lax.ppermute(theirs, ("member", "sub"), along(False)))
    visc = jnp.concatenate([stats[comps] for stats in stats_mine], 0)
    visc_got = lax.ppermute(visc, ("member", "sub"), along(True))
    visc_other = lax.ppermute(visc_got, "member", swap)

    early = EARLY
    n_early = sum(1 for piece in PIECES if piece[1] <= early)
    width = depth - early
    coef, scaled, edges, middle = call(
        functools.partial(early_kernel, PIECES, early, sizes, nx),
        [
            (7, nx + 2 * depth, *layer),
            (comps, nx + 2 * depth, *layer),
            (depth, 2, comps, 2, *layer),
            (comps, nx - 2 * width, ny, nz),
        ],
        src_mine + src_theirs + stats_mine + stats_theirs + [visc_got, visc_other]
        + halo_mine[:n_early] + halo_theirs[:n_early],
        20 * 8 * velocity.size,
        scratch=[
            pltpu.VMEM((nx + 2 * depth, *layer), f32),
            pltpu.VMEM((depth + 1, comps, nx + 2 * early, *layer), f32),
        ],
        name="early",
    )
    return call(
        functools.partial(late_kernel, PIECES, early, sizes, nx),
        [velocity.shape],
        [coef, scaled, edges, middle] + halo_mine[n_early:] + halo_theirs[n_early:],
        20 * 4 * velocity.size,
        scratch=[
            pltpu.VMEM((depth + 1, 2, comps, width + 2, *layer), f32),
            pltpu.VMEM((2, comps, 2 * depth, *layer), f32),
            pltpu.VMEM((2, comps, width, ny, nz), f32),
            pltpu.SemaphoreType.DMA((3,)),
        ],
        any_out=True,
        name="late",
    )[0]


def solution(mesh):
    in_specs = (P("member", None, "sub", None, None), P("member", None, "sub", None, None))
    out_specs = P("member", None, "sub", None, None)
    return jax.shard_map(fast, mesh=mesh, in_specs=in_specs, out_specs=out_specs, check_vma=False)
```

```python
import functools
import math

import jax
import jax.numpy as jnp
from jax import lax
from jax.experimental import pallas as pl
from jax.experimental.pallas import tpu as pltpu
from jax.sharding import PartitionSpec as P

SWEEPS = 8


TIME_STEP = 0.25
EDDY_COEFF = 1.0
BASE_VISCOSITY = 1.0
LOWER_EDGE = 0.1
UPPER_EDGE = 1.9

ROWS = 8
PIECES = ((0, 4), (4, 8))
STAGES = ((0, 4), (4, 8))
OWN = True
GATE = True
PAD = 1
TIE = False
SINGLE = False
FAKE = 11
WEIGHT = {}
VMEM_LIMIT = 40 * 1024 * 1024


def step_sizes(sweep_count):
    middle = (UPPER_EDGE + LOWER_EDGE) / 2
    radius = (UPPER_EDGE - LOWER_EDGE) / 2
    return [
        1.0 / (middle + radius * math.cos(math.pi * (2 * position + 1) / (2 * sweep_count)))
        for position in range(sweep_count)
    ]


def north(planes, j):
    return planes[j + 1] if j + 1 < len(planes) else pltpu.roll(planes[0], ROWS - 1, 0)


def south(planes, j):
    return planes[j - 1] if j else pltpu.roll(planes[-1], 1, 0)


def upper(plane):
    return pltpu.roll(plane, plane.shape[-1] - 1, 1)


def lower(plane):
    return pltpu.roll(plane, 1, 1)


def rows_of(j, count):
    return pl.ds(j, ROWS, stride=count)


def parity():
    return lax.rem(lax.axis_index("member"), 2)


def for_layers(count, body, unroll=1):
    def step(i, carry):
        body(i)
        return carry

    lax.fori_loop(0, count, step, 0, unroll=unroll)


def arrange_kernel(vel, force, vp, gp, first, last):
    comps, nx, planes = vp.shape[:3]

    def body(x):
        for c in range(comps):
            for j in range(planes):
                value = vel[0, c, x, rows_of(j, planes), :]
                vp[c, x, j] = value
                gp[c, x, j] = value + TIME_STEP * force[0, c, x, rows_of(j, planes), :]

    for_layers(nx, body, 2)
    first[...] = vp[:, :1]
    last[...] = vp[:, nx - 1 :]


def sums_kernel(pieces, vp, other, *refs):
    outs = refs[len(refs) - len(pieces) :]
    comps, nx, planes = vp.shape[:3]
    side = parity()
    for (near, far), out in zip(pieces, outs):
        start = jnp.where(side == 0, near, nx - far)

        def body(i, out=out, start=start):
            x = start + i
            for j in range(planes):
                squares = None
                for c in range(comps):
                    a = vp[c, x, j]
                    b = other[0, c, x, rows_of(j, planes), :]
                    out[c, i, j] = a + b
                    both = a * a + b * b
                    squares = both if squares is None else squares + both
                out[comps, i, j] = squares

        for_layers(far - near, body)


def add_kernel(*refs):
    refs[-1][...] = refs[0][...] + refs[1][...]


def gate_kernel(*refs):
    count = refs[0].shape[0]
    refs[-1][:count] = refs[0][...]


def stats_kernel(members, add_two, *refs):
    flow, rest = refs[-2:]
    comps, layers, planes = refs[0].shape[0] - 1, refs[0].shape[1], refs[0].shape[2]

    def body(i):
        for j in range(planes):
            def total(c):
                value = refs[0][c, i, j]
                return value + refs[1][c, i, j] if add_two else value

            spread = total(comps) * (1.0 / members)
            for c in range(comps):
                mean = total(c) * (1.0 / members)
                if c < comps - 1:
                    flow[c, i, j] = mean
                else:
                    rest[0, i, j] = mean
                spread = spread - mean * mean
            rest[1, i, j] = BASE_VISCOSITY + EDDY_COEFF * TIME_STEP * spread

    for_layers(layers, body)


def source_kernel(piece, vp, gp, below, above, mine, mine_rest, theirs, theirs_rest, *refs):
    out_mine, out_theirs = refs[-2:]
    comps, nx, planes = vp.shape[:3]
    near, far = piece
    side = parity()
    for which, stats, rest, out in (
        (side, mine, mine_rest, out_mine),
        (1 - side, theirs, theirs_rest, out_theirs),
    ):
        start = jnp.where(which == 0, near, nx - far)

        def body(i, stats=stats, rest=rest, out=out, start=start):
            x = start + i
            down, up = jnp.maximum(x - 1, 0), jnp.minimum(x + 1, nx - 1)
            for c in range(comps):
                here = [vp[c, x, j] for j in range(planes)]
                for j in range(planes):
                    west = jnp.where(x == 0, below[c, 0, j], vp[c, down, j])
                    east = jnp.where(x == nx - 1, above[c, 0, j], vp[c, up, j])
                    transport = (
                        stats[0, i, j] * (east - west)
                        + stats[1, i, j] * (north(here, j) - south(here, j))
                        + rest[0, i, j] * (upper(here[j]) - lower(here[j]))
                    )
                    out[c, i, j] = gp[c, x, j] - (0.5 * TIME_STEP) * transport

        for_layers(far - near, body, far - near)


def relaxed(center, outward, inward, coef, source, comps, planes, step_size):
    here = [[center(c, j) for j in range(planes)] for c in range(comps)]
    values = []
    for j in range(planes):
        faces = [coef(a, j) for a in range(6)]
        for c in range(comps):
            ns, ss = north(here[c], j), south(here[c], j)
            image = source(c, j) + faces[0] * inward(c, j)
            image = image + faces[1] * outward(c, j)
            image = image + (faces[2] * ns + faces[3] * ss)
            image = image + (faces[4] * upper(here[c][j]) + faces[5] * lower(here[c][j]))
            values.append((c, j, (1.0 - step_size) * here[c][j] + step_size * image))
    return values


class Taker:
    def __init__(self, refs):
        self.refs, self.at = refs, 0

    def __call__(self, n=1):
        self.at += n
        return list(self.refs[self.at - n : self.at])


def make_coefs(visc_here, visc_in, visc_out, put, planes):
    half = 0.5 * TIME_STEP
    for j in range(planes):
        here = visc_here[j]
        faces = [
            here + visc_in[j],
            here + visc_out[j],
            here + north(visc_here, j),
            here + south(visc_here, j),
            here + upper(here),
            here + lower(here),
        ]
        total = (faces[0] + faces[1]) + (faces[2] + faces[3]) + (faces[4] + faces[5])
        inverse = 1.0 / (1.0 + half * total)
        scale = half * inverse
        for a in range(6):
            put(a, j, faces[a] * scale)
        put(6, j, inverse)


def run_sweeps(reach, before, sizes, comps, planes, load, coef, source, keep, last):
    depth = len(sizes)
    for k in range(1, depth + 1):
        layers = range(k + depth - reach, min(k + depth - before, 2 * depth))
        for s in range(2):
            found = []
            for i in layers:
                found.append(
                    relaxed(
                        lambda c, j: load(k - 1, s, c, i, j),
                        lambda c, j: load(k - 1, s, c, i - 1, j),
                        lambda c, j: load(k - 1, s, c, i + 1, j),
                        lambda a, j: coef(s, a, i, j),
                        lambda c, j: source(s, c, i, j),
                        comps,
                        planes,
                        sizes[k - 1],
                    )
                )
            for i, values in zip(layers, found):
                for c, j, value in values:
                    if k < depth:
                        keep(k, s, c, i, j, value)
                    else:
                        last(s, c, i, j, value)


def own_kernel(pieces, sizes, count, *refs):
    number = len(pieces)
    take = Taker(refs)
    src_mine, src_theirs = take(number), take(number)
    stat_mine, stat_theirs = take(number), take(number)
    coef, scaled, edges, visc = take(4)
    (field,) = take(1)
    depth = len(sizes)
    comps, planes = scaled.shape[1], scaled.shape[3]
    side = parity()
    for which, stats, srcs in ((side, stat_mine, src_mine), (1 - side, stat_theirs, src_theirs)):
        for (near, far), stat, src in zip(pieces, stats, srcs):
            for e in range(far - near):
                d = jnp.where(which == 0, near + e, far - 1 - e)
                visc[which, d] = stat[1, e]
                for c in range(comps):
                    field[0, which, c, d] = src[c, e]
    for s in range(2):
        for d in range(1, depth):
            def put(a, j, value):
                coef[s, a, d, j] = value

            make_coefs(
                [visc[s, d, j] for j in range(planes)],
                [visc[s, d + 1, j] if d + 1 < depth else visc[1 - s, d, j] for j in range(planes)],
                [visc[s, d - 1, j] for j in range(planes)],
                put,
                planes,
            )
            for c in range(comps):
                for j in range(planes):
                    scaled[s, c, d, j] = field[0, s, c, d, j] * coef[s, 6, d, j]

    def load(k, s, c, i, j):
        return field[k, s, c, i - depth, j] if i < 2 * depth else field[k, 1 - s, c, depth - 1, j]

    def keep(k, s, c, i, j, value):
        field[k, s, c, i - depth, j] = value

    triangle(sizes, comps, planes, load, coef, scaled, keep)
    for k in range(depth):
        for s in range(2):
            for c in range(comps):
                edges[k, s, c, 0] = field[k, s, c, k]
                edges[k, s, c, 1] = (
                    field[k, s, c, k + 1] if k + 1 < depth else field[k, 1 - s, c, depth - 1]
                )


def triangle(sizes, comps, planes, load, coef, scaled, keep):
    depth = len(sizes)
    for k in range(1, depth):
        for s in range(2):
            layers = range(k + depth, 2 * depth)
            found = [
                relaxed(
                    lambda c, j: load(k - 1, s, c, i, j),
                    lambda c, j: load(k - 1, s, c, i - 1, j),
                    lambda c, j: load(k - 1, s, c, i + 1, j),
                    lambda a, j: coef[s, a, i - depth, j],
                    lambda c, j: scaled[s, c, i - depth, j],
                    comps,
                    planes,
                    sizes[k - 1],
                )
                for i in layers
            ]
            for i, values in zip(layers, found):
                for c, j, value in values:
                    keep(k, s, c, i, j, value)


def stage_kernel(pieces, piece, first, final, sizes, count, olds, *refs):
    take = Taker(refs)
    depth = len(sizes)
    near, far = piece
    width = far - near
    (coef_own,) = take()
    if first:
        visc_own, visc_got, visc_other = take(3)
    else:
        (coef_halo,) = take()
    scaled_own = take()[0]
    scaled_old = take(len(olds))
    edges_in, halo_mine, halo_theirs = take(3)
    if final:
        parts = take(len(olds))
        (out,) = take()
    else:
        scaled_new, edges, part = take(3)
        if first:
            (coef_halo,) = take()
    (field,) = take()
    if first:
        (visc,) = take()
    if final:
        scaled_new, tail, sems = take(3)
    comps, planes = scaled_own.shape[1], scaled_own.shape[3]
    side = parity()

    copies = []
    if final:
        for n, ((lo, hi), done) in enumerate(zip(olds, parts)):
            for s in range(2):
                where = depth - hi if s == 0 else count - depth + lo
                copies.append(
                    pltpu.make_async_copy(
                        done.at[s], out.at[0, :, where : where + hi - lo], sems.at[2 * n + s]
                    )
                )
                copies[-1].start()

    for which, halo in ((side, halo_mine), (1 - side, halo_theirs)):
        for e in range(width):
            spot = jnp.where(which == 0, width - 1 - e, e)
            for c in range(comps):
                field[0, 1 - which, c, spot] = halo[c, e]
    for k in range(depth):
        for s in range(2):
            for c in range(comps):
                for e in range(2):
                    field[k, s, c, width + e] = edges_in[k, s, c, e]

    if first:
        for which, got in ((side, visc_got), (1 - side, visc_other)):
            for lo, hi in pieces:
                for e in range(hi - lo):
                    i = jnp.where(which == 0, depth - 1 - lo - e, depth - hi + e)
                    visc[1 - which, i] = got[lo + e]
        for s in range(2):
            for d in range(2):
                visc[s, depth + d] = visc_own[s, d]
        for s in range(2):
            for i in range(1, depth + 1):
                def put(a, j, value):
                    coef_halo[s, a, i, j] = value

                make_coefs(
                    [visc[s, i, j] for j in range(planes)],
                    [visc[s, i + 1, j] for j in range(planes)],
                    [visc[s, i - 1, j] for j in range(planes)],
                    put,
                    planes,
                )

    def coef(s, a, i, j):
        return coef_halo[s, a, i, j] if i <= depth else coef_own[s, a, i - depth, j]

    base = depth - far
    for s in range(2):
        for p in range(width):
            i = base + p
            if i > 0:
                for c in range(comps):
                    for j in range(planes):
                        scaled_new[s, c, p, j] = field[0, s, c, p, j] * coef_halo[s, 6, i, j]
        if first:
            for c in range(comps):
                for j in range(planes):
                    scaled_new[s, c, width, j] = edges_in[0, s, c, 0, j] * coef_halo[s, 6, depth, j]

    def source(s, c, i, j):
        if i > depth:
            return scaled_own[s, c, i - depth, j]
        if first:
            return scaled_new[s, c, i - base, j]
        if i == depth:
            lo, hi = olds[0]
            return scaled_old[0][s, c, hi - lo, j]
        d = depth - 1 - i
        if near <= d < far:
            return scaled_new[s, c, i - base, j]
        for (lo, hi), ref in zip(olds, scaled_old):
            if lo <= d < hi:
                return ref[s, c, i - (depth - hi), j]
        raise ValueError("no source")

    def load(k, s, c, i, j):
        return field[k, s, c, i - (k + depth - far), j]

    def keep(k, s, c, i, j, value):
        field[k, s, c, i - (k + depth - far), j] = value

    def last(s, c, i, j, value):
        p = i - (2 * depth - far)
        place = p if s == 0 else width - 1 - p
        target = tail if final else part
        target[s, c, place, rows_of(j, planes), :] = value

    run_sweeps(far, near, sizes, comps, planes, load, coef, source, keep, last)

    if final:
        for s in range(2):
            where = depth - far if s == 0 else count - depth + near
            copies.append(
                pltpu.make_async_copy(
                    tail.at[s], out.at[0, :, where : where + width], sems.at[2 * len(olds) + s]
                )
            )
            copies[-1].start()
        for copy in copies:
            copy.wait()
    else:
        for k in range(depth):
            for s in range(2):
                for c in range(comps):
                    for e in range(2):
                        edges[k, s, c, e] = field[k, s, c, e]


def vmem(n):
    return [pl.BlockSpec(memory_space=pltpu.VMEM)] * n


def call(kernel, outs, ins, flops, scratch=(), any_out=False, name=None):
    shapes = [jax.ShapeDtypeStruct(shape, jnp.float32) for shape in outs]
    size = int(3.7e6 * WEIGHT[name]) if name in WEIGHT else 4 * sum(math.prod(shape) for shape in outs) + 4 * sum(x.size for x in ins)
    flops = 0 if name in WEIGHT else flops
    result = pl.pallas_call(
        kernel,
        out_shape=shapes,
        in_specs=vmem(len(ins)),
        out_specs=[pl.BlockSpec(memory_space=pl.ANY)] * len(outs) if any_out else vmem(len(outs)),
        scratch_shapes=list(scratch),
        compiler_params=pltpu.CompilerParams(vmem_limit_bytes=VMEM_LIMIT),
        cost_estimate=pl.CostEstimate(flops=flops, bytes_accessed=size, transcendentals=0),
        name=name,
    )(*ins)
    return result


def fast(velocity, forcing):
    members = lax.axis_size("member")
    subs = lax.axis_size("sub")
    _, comps, nx, ny, nz = velocity.shape
    planes = ny // ROWS
    layer = (planes, ROWS, nz)
    sizes = step_sizes(SWEEPS)
    depth = SWEEPS
    bits = members.bit_length() - 1
    f32 = jnp.float32

    swap = [(m, m ^ 1) for m in range(members)]

    def pair(step):
        order = [list(range(1, bits)), list(range(2, bits)) + [1]]
        return [(m, m ^ (1 << order[m % 2][step])) for m in range(members)]

    def along(mine):
        moves = []
        for m in range(members):
            step = -1 if (m % 2 == 0) == mine else 1
            for s in range(subs):
                moves.append((m * subs + s, m * subs + (s + step) % subs))
        return moves

    other = lax.ppermute(velocity, "member", swap)
    vp, gp, first, last = call(
        arrange_kernel,
        [(comps, nx, *layer)] * 2 + [(comps, 1, *layer)] * 2,
        [velocity, forcing],
        10 * velocity.size,
        name="arrange",
    )
    above = lax.ppermute(first, "sub", [(s, (s - 1) % subs) for s in range(subs)])
    below = lax.ppermute(last, "sub", [(s, (s + 1) % subs) for s in range(subs)])
    hold = []
    if FAKE:
        hold = call(gate_kernel, [(FAKE, 1, *layer)], [below, above], 1, name="gate")
        hold = [lax.ppermute(hold[0], "member", swap)]
    parts = list(call(
        functools.partial(sums_kernel, PIECES),
        [(comps + 1, far - near, *layer) for near, far in PIECES],
        [vp, other],
        6 * velocity.size,
        name="sums",
    ))
    got = [None] * len(parts)
    for step in range(bits - 1):
        for i, part in enumerate(parts):
            if step:
                tie = [parts[i - 1]] if i else []
                if i and step == 1:
                    tie += hold or [below, above]
                parts[i] = part = call(
                    add_kernel, [part.shape], [part, got[i]] + tie, part.size, name="add%d" % i
                )[0]
            got[i] = lax.ppermute(part, "member", pair(step))
    stats_mine, stats_theirs, src_mine, src_theirs, halo_mine, halo_theirs = [], [], [], [], [], []
    tie = parts[1:]
    for i, ((near, far), part, last_got) in enumerate(zip(PIECES, parts, got)):
        terms = [part] if last_got is None else [part, last_got]
        stats = call(
            functools.partial(stats_kernel, members, len(terms) == 2),
            [(comps - 1, far - near, *layer), (2, far - near, *layer)],
            terms + tie,
            10 * part.size,
            name="stats%d" % i,
        )
        swapped = [lax.ppermute(x, "member", swap) for x in stats]
        if SINGLE:
            swapped = [jnp.concatenate([lax.ppermute(x[:1], "member", swap), lax.ppermute(x[1:], "member", swap)]) for x in stats]
        stats_mine.append(stats[1])
        stats_theirs.append(swapped[1])
        mine, theirs = call(
            functools.partial(source_kernel, (near, far)),
            [(comps, far - near, *layer)] * 2,
            [vp, gp, below, above, *stats, *swapped],
            20 * part.size,
            name="source%d" % i,
        )
        mines, theirses = [mine], [theirs]
        src_mine.append(mine)
        src_theirs.append(theirs)
        for mine_part, theirs_part in zip(mines, theirses):
            halo_mine.append(lax.ppermute(mine_part, ("member", "sub"), along(True)))
            halo_theirs.append(lax.ppermute(theirs_part, ("member", "sub"), along(False)))
        tie = [mine]
    visc = jnp.concatenate([rest[1] for rest in stats_mine], 0)
    visc_got = lax.ppermute(visc, ("member", "sub"), along(True))
    own = call(
        functools.partial(own_kernel, PIECES, sizes, nx),
        [(2, 7, depth, *layer), (2, comps, depth, *layer), (depth, 2, comps, 2, *layer), (2, depth, *layer)],
        src_mine + src_theirs + stats_mine + stats_theirs,
        20 * 3 * velocity.size,
        scratch=[pltpu.VMEM((depth, 2, comps, depth, *layer), f32)],
        name="own",
    )
    coef_own, scaled_own, edges, visc_own = own
    if GATE:
        tie = [src_mine[-1]] if TIE else []
        visc_got = call(
            gate_kernel,
            [(PAD + depth, *layer)],
            [visc_got, halo_mine[0], halo_theirs[0]] + tie + ([edges] if OWN else []),
            1,
            name="gate",
        )[0]
    visc_other = lax.ppermute(visc_got, "member", swap)
    olds, scaled_old, parts = [], [], []
    for n, (piece, mine, theirs) in enumerate(zip(STAGES, halo_mine, halo_theirs)):
        first, final = n == 0, n == len(STAGES) - 1
        width = piece[1] - piece[0]
        ins = [coef_own]
        ins += [visc_own, visc_got, visc_other] if first else [coef_halo]
        ins += [scaled_own] + scaled_old + [edges, mine, theirs]
        scratch = [pltpu.VMEM((depth, 2, comps, width + 2, *layer), f32)]
        if first:
            scratch.append(pltpu.VMEM((2, depth + 2, *layer), f32))
        if final:
            ins += parts
            outs = [velocity.shape]
            scratch += [
                pltpu.VMEM((2, comps, width, *layer), f32),
                pltpu.VMEM((2, comps, width, ny, nz), f32),
                pltpu.SemaphoreType.DMA((2 * len(STAGES),)),
            ]
        else:
            outs = [
                (2, comps, width + 1, *layer),
                (depth, 2, comps, 2, *layer),
                (2, comps, width, ny, nz),
            ]
            if first:
                outs.append((2, 7, depth + 1, *layer))
        results = call(
            functools.partial(stage_kernel, PIECES, piece, first, final, sizes, nx, list(olds)),
            outs,
            ins,
            20 * width * velocity.size,
            scratch=scratch,
            any_out=final,
            name="stage%d" % n,
        )
        if final:
            return results[0]
        if first:
            coef_halo = results[3]
        olds.append(piece)
        scaled_old.append(results[0])
        edges = results[1]
        parts.append(results[2])


def solution(mesh):
    in_specs = (P("member", None, "sub", None, None), P("member", None, "sub", None, None))
    out_specs = P("member", None, "sub", None, None)
    return jax.shard_map(fast, mesh=mesh, in_specs=in_specs, out_specs=out_specs, check_vma=False)
```

```python
import functools
import math

import jax
import jax.numpy as jnp
from jax import lax
from jax.experimental import pallas as pl
from jax.experimental.pallas import tpu as pltpu
from jax.sharding import PartitionSpec as P

SWEEPS = 8


TIME_STEP = 0.25
EDDY_COEFF = 1.0
BASE_VISCOSITY = 1.0
LOWER_EDGE = 0.1
UPPER_EDGE = 1.9

ROWS = 8
PIECES = ((0, 4), (4, 8))
STAGES = ((0, 4), (4, 8))
PAD = 5
FAKE = 9
VMEM_LIMIT = 40 * 1024 * 1024


def step_sizes(sweep_count):
    middle = (UPPER_EDGE + LOWER_EDGE) / 2
    radius = (UPPER_EDGE - LOWER_EDGE) / 2
    return [
        1.0 / (middle + radius * math.cos(math.pi * (2 * position + 1) / (2 * sweep_count)))
        for position in range(sweep_count)
    ]


def north(planes, j):
    return planes[j + 1] if j + 1 < len(planes) else pltpu.roll(planes[0], ROWS - 1, 0)


def south(planes, j):
    return planes[j - 1] if j else pltpu.roll(planes[-1], 1, 0)


def upper(plane):
    return pltpu.roll(plane, plane.shape[-1] - 1, 1)


def lower(plane):
    return pltpu.roll(plane, 1, 1)


def rows_of(j, count):
    return pl.ds(j, ROWS, stride=count)


def parity():
    return lax.rem(lax.axis_index("member"), 2)


def for_layers(count, body, unroll=1):
    def step(i, carry):
        body(i)
        return carry

    lax.fori_loop(0, count, step, 0, unroll=unroll)


def arrange_kernel(vel, force, vp, gp, first, last):
    comps, nx, planes = vp.shape[:3]

    def body(x):
        for c in range(comps):
            for j in range(planes):
                value = vel[0, c, x, rows_of(j, planes), :]
                vp[c, x, j] = value
                gp[c, x, j] = value + TIME_STEP * force[0, c, x, rows_of(j, planes), :]

    for_layers(nx, body, 2)
    first[...] = vp[:, :1]
    last[...] = vp[:, nx - 1 :]


def sums_kernel(pieces, vp, other, *refs):
    outs = refs[len(refs) - len(pieces) :]
    comps, nx, planes = vp.shape[:3]
    side = parity()
    for (near, far), out in zip(pieces, outs):
        start = jnp.where(side == 0, near, nx - far)

        def body(i, out=out, start=start):
            x = start + i
            for j in range(planes):
                squares = None
                for c in range(comps):
                    a = vp[c, x, j]
                    b = other[0, c, x, rows_of(j, planes), :]
                    out[c, i, j] = a + b
                    both = a * a + b * b
                    squares = both if squares is None else squares + both
                out[comps, i, j] = squares

        for_layers(far - near, body)


def add_kernel(*refs):
    refs[-1][...] = refs[0][...] + refs[1][...]


def quarter():
    return lax.rem(lax.axis_index("member") // 2, 2)


def gate_kernel(*refs):
    count = refs[0].shape[0]
    refs[-1][:count] = refs[0][...]


def share_kernel(*refs):
    count = refs[0].shape[0]
    refs[-2][...] = refs[0][...]
    refs[-1][:count] = refs[0][...]


def pick_kernel(first, second, out):
    out[...] = jnp.where(quarter() == 0, first[1], second[1])


def stats_kernel(members, add_two, *refs):
    flow, rest = refs[-2:]
    comps, layers, planes = refs[0].shape[0] - 1, refs[0].shape[1], refs[0].shape[2]

    def body(i):
        for j in range(planes):
            def total(c):
                value = refs[0][c, i, j]
                return value + refs[1][c, i, j] if add_two else value

            spread = total(comps) * (1.0 / members)
            for c in range(comps):
                mean = total(c) * (1.0 / members)
                if c < comps - 1:
                    flow[c, i, j] = mean
                else:
                    rest[0, i, j] = mean
                spread = spread - mean * mean
            rest[1, i, j] = BASE_VISCOSITY + EDDY_COEFF * TIME_STEP * spread

    for_layers(layers, body)


def source_kernel(piece, vp, gp, below, above, mine, mine_rest, theirs, theirs_rest, *refs):
    out_mine, out_theirs = refs[-2:]
    comps, nx, planes = vp.shape[:3]
    near, far = piece
    side = parity()
    for which, stats, rest, out in (
        (side, mine, mine_rest, out_mine),
        (1 - side, theirs, theirs_rest, out_theirs),
    ):
        start = jnp.where(which == 0, near, nx - far)

        def body(i, stats=stats, rest=rest, out=out, start=start):
            x = start + i
            down, up = jnp.maximum(x - 1, 0), jnp.minimum(x + 1, nx - 1)
            for c in range(comps):
                here = [vp[c, x, j] for j in range(planes)]
                for j in range(planes):
                    west = jnp.where(x == 0, below[c, 0, j], vp[c, down, j])
                    east = jnp.where(x == nx - 1, above[c, 0, j], vp[c, up, j])
                    transport = (
                        stats[0, i, j] * (east - west)
                        + stats[1, i, j] * (north(here, j) - south(here, j))
                        + rest[0, i, j] * (upper(here[j]) - lower(here[j]))
                    )
                    out[c, i, j] = gp[c, x, j] - (0.5 * TIME_STEP) * transport

        for_layers(far - near, body, far - near)


def relaxed(center, outward, inward, coef, source, comps, planes, step_size):
    here = [[center(c, j) for j in range(planes)] for c in range(comps)]
    values = []
    for j in range(planes):
        faces = [coef(a, j) for a in range(6)]
        for c in range(comps):
            ns, ss = north(here[c], j), south(here[c], j)
            image = source(c, j) + faces[0] * inward(c, j)
            image = image + faces[1] * outward(c, j)
            image = image + (faces[2] * ns + faces[3] * ss)
            image = image + (faces[4] * upper(here[c][j]) + faces[5] * lower(here[c][j]))
            values.append((c, j, (1.0 - step_size) * here[c][j] + step_size * image))
    return values


class Taker:
    def __init__(self, refs):
        self.refs, self.at = refs, 0

    def __call__(self, n=1):
        self.at += n
        return list(self.refs[self.at - n : self.at])


def make_coefs(visc_here, visc_in, visc_out, put, planes):
    half = 0.5 * TIME_STEP
    for j in range(planes):
        here = visc_here[j]
        faces = [
            here + visc_in[j],
            here + visc_out[j],
            here + north(visc_here, j),
            here + south(visc_here, j),
            here + upper(here),
            here + lower(here),
        ]
        total = (faces[0] + faces[1]) + (faces[2] + faces[3]) + (faces[4] + faces[5])
        inverse = 1.0 / (1.0 + half * total)
        scale = half * inverse
        for a in range(6):
            put(a, j, faces[a] * scale)
        put(6, j, inverse)


def run_sweeps(reach, before, sizes, comps, planes, load, coef, source, keep, last):
    depth = len(sizes)
    for k in range(1, depth + 1):
        layers = range(k + depth - reach, min(k + depth - before, 2 * depth))
        for s in range(2):
            found = []
            for i in layers:
                found.append(
                    relaxed(
                        lambda c, j: load(k - 1, s, c, i, j),
                        lambda c, j: load(k - 1, s, c, i - 1, j),
                        lambda c, j: load(k - 1, s, c, i + 1, j),
                        lambda a, j: coef(s, a, i, j),
                        lambda c, j: source(s, c, i, j),
                        comps,
                        planes,
                        sizes[k - 1],
                    )
                )
            for i, values in zip(layers, found):
                for c, j, value in values:
                    if k < depth:
                        keep(k, s, c, i, j, value)
                    else:
                        last(s, c, i, j, value)


def own_kernel(pieces, sizes, count, *refs):
    number = len(pieces)
    take = Taker(refs)
    src_mine, src_theirs = take(number), take(number)
    stat_mine, stat_theirs = take(number), take(number)
    coef, scaled, edges, visc = take(4)
    (field,) = take(1)
    depth = len(sizes)
    comps, planes = scaled.shape[1], scaled.shape[3]
    side = parity()
    for which, stats, srcs in ((side, stat_mine, src_mine), (1 - side, stat_theirs, src_theirs)):
        for (near, far), stat, src in zip(pieces, stats, srcs):
            for e in range(far - near):
                d = jnp.where(which == 0, near + e, far - 1 - e)
                visc[which, d] = stat[1, e]
                for c in range(comps):
                    field[0, which, c, d] = src[c, e]
    for s in range(2):
        for d in range(1, depth):
            def put(a, j, value):
                coef[s, a, d, j] = value

            make_coefs(
                [visc[s, d, j] for j in range(planes)],
                [visc[s, d + 1, j] if d + 1 < depth else visc[1 - s, d, j] for j in range(planes)],
                [visc[s, d - 1, j] for j in range(planes)],
                put,
                planes,
            )
            for c in range(comps):
                for j in range(planes):
                    scaled[s, c, d, j] = field[0, s, c, d, j] * coef[s, 6, d, j]

    def load(k, s, c, i, j):
        return field[k, s, c, i - depth, j] if i < 2 * depth else field[k, 1 - s, c, depth - 1, j]

    def keep(k, s, c, i, j, value):
        field[k, s, c, i - depth, j] = value

    triangle(sizes, comps, planes, load, coef, scaled, keep)
    for k in range(depth):
        for s in range(2):
            for c in range(comps):
                edges[k, s, c, 0] = field[k, s, c, k]
                edges[k, s, c, 1] = (
                    field[k, s, c, k + 1] if k + 1 < depth else field[k, 1 - s, c, depth - 1]
                )


def triangle(sizes, comps, planes, load, coef, scaled, keep):
    depth = len(sizes)
    for k in range(1, depth):
        for s in range(2):
            layers = range(k + depth, 2 * depth)
            found = [
                relaxed(
                    lambda c, j: load(k - 1, s, c, i, j),
                    lambda c, j: load(k - 1, s, c, i - 1, j),
                    lambda c, j: load(k - 1, s, c, i + 1, j),
                    lambda a, j: coef[s, a, i - depth, j],
                    lambda c, j: scaled[s, c, i - depth, j],
                    comps,
                    planes,
                    sizes[k - 1],
                )
                for i in layers
            ]
            for i, values in zip(layers, found):
                for c, j, value in values:
                    keep(k, s, c, i, j, value)


def stage_kernel(pieces, piece, first, final, sizes, count, olds, *refs):
    take = Taker(refs)
    depth = len(sizes)
    near, far = piece
    width = far - near
    (coef_own,) = take()
    if first:
        (visc_own,) = take()
        visc_halo = take(4)
    else:
        (coef_halo,) = take()
    scaled_own = take()[0]
    scaled_old = take(len(olds))
    edges_in, halo_mine, halo_theirs = take(3)
    if final:
        parts = take(len(olds))
        (out,) = take()
    else:
        scaled_new, edges, part = take(3)
        if first:
            (coef_halo,) = take()
    (field,) = take()
    if first:
        (visc,) = take()
    if final:
        scaled_new, tail, sems = take(3)
    comps, planes = scaled_own.shape[1], scaled_own.shape[3]
    side = parity()

    copies = []
    if final:
        for n, ((lo, hi), done) in enumerate(zip(olds, parts)):
            for s in range(2):
                where = depth - hi if s == 0 else count - depth + lo
                copies.append(
                    pltpu.make_async_copy(
                        done.at[s], out.at[0, :, where : where + hi - lo], sems.at[2 * n + s]
                    )
                )
                copies[-1].start()

    for which, halo in ((side, halo_mine), (1 - side, halo_theirs)):
        for e in range(width):
            spot = jnp.where(which == 0, width - 1 - e, e)
            for c in range(comps):
                field[0, 1 - which, c, spot] = halo[c, e]
    for k in range(depth):
        for s in range(2):
            for c in range(comps):
                for e in range(2):
                    field[k, s, c, width + e] = edges_in[k, s, c, e]

    if first:
        length = pieces[0][1] - pieces[0][0]
        for hop, got in enumerate(visc_halo):
            which = side if hop % 2 == 0 else 1 - side
            lo = length * (quarter() if hop < 2 else 1 - quarter())
            for e in range(length):
                i = jnp.where(which == 0, depth - 1 - lo - e, depth - lo - length + e)
                visc[1 - which, i] = got[e]
        for s in range(2):
            for d in range(2):
                visc[s, depth + d] = visc_own[s, d]
        for s in range(2):
            for i in range(1, depth + 1):
                def put(a, j, value):
                    coef_halo[s, a, i, j] = value

                make_coefs(
                    [visc[s, i, j] for j in range(planes)],
                    [visc[s, i + 1, j] for j in range(planes)],
                    [visc[s, i - 1, j] for j in range(planes)],
                    put,
                    planes,
                )

    def coef(s, a, i, j):
        return coef_halo[s, a, i, j] if i <= depth else coef_own[s, a, i - depth, j]

    base = depth - far
    for s in range(2):
        for p in range(width):
            i = base + p
            if i > 0:
                for c in range(comps):
                    for j in range(planes):
                        scaled_new[s, c, p, j] = field[0, s, c, p, j] * coef_halo[s, 6, i, j]
        if first:
            for c in range(comps):
                for j in range(planes):
                    scaled_new[s, c, width, j] = edges_in[0, s, c, 0, j] * coef_halo[s, 6, depth, j]

    def source(s, c, i, j):
        if i > depth:
            return scaled_own[s, c, i - depth, j]
        if first:
            return scaled_new[s, c, i - base, j]
        if i == depth:
            lo, hi = olds[0]
            return scaled_old[0][s, c, hi - lo, j]
        d = depth - 1 - i
        if near <= d < far:
            return scaled_new[s, c, i - base, j]
        for (lo, hi), ref in zip(olds, scaled_old):
            if lo <= d < hi:
                return ref[s, c, i - (depth - hi), j]
        raise ValueError("no source")

    def load(k, s, c, i, j):
        return field[k, s, c, i - (k + depth - far), j]

    def keep(k, s, c, i, j, value):
        field[k, s, c, i - (k + depth - far), j] = value

    def last(s, c, i, j, value):
        p = i - (2 * depth - far)
        place = p if s == 0 else width - 1 - p
        target = tail if final else part
        target[s, c, place, rows_of(j, planes), :] = value

    run_sweeps(far, near, sizes, comps, planes, load, coef, source, keep, last)

    if final:
        for s in range(2):
            where = depth - far if s == 0 else count - depth + near
            copies.append(
                pltpu.make_async_copy(
                    tail.at[s], out.at[0, :, where : where + width], sems.at[2 * len(olds) + s]
                )
            )
            copies[-1].start()
        for copy in copies:
            copy.wait()
    else:
        for k in range(depth):
            for s in range(2):
                for c in range(comps):
                    for e in range(2):
                        edges[k, s, c, e] = field[k, s, c, e]


def vmem(n):
    return [pl.BlockSpec(memory_space=pltpu.VMEM)] * n


def call(kernel, outs, ins, flops, scratch=(), any_out=False, name=None):
    shapes = [jax.ShapeDtypeStruct(shape, jnp.float32) for shape in outs]
    size = 4 * sum(math.prod(shape) for shape in outs) + 4 * sum(x.size for x in ins)
    result = pl.pallas_call(
        kernel,
        out_shape=shapes,
        in_specs=vmem(len(ins)),
        out_specs=[pl.BlockSpec(memory_space=pl.ANY)] * len(outs) if any_out else vmem(len(outs)),
        scratch_shapes=list(scratch),
        compiler_params=pltpu.CompilerParams(vmem_limit_bytes=VMEM_LIMIT),
        cost_estimate=pl.CostEstimate(flops=flops, bytes_accessed=size, transcendentals=0),
        name=name,
    )(*ins)
    return result


def fast(velocity, forcing):
    members = lax.axis_size("member")
    subs = lax.axis_size("sub")
    _, comps, nx, ny, nz = velocity.shape
    planes = ny // ROWS
    layer = (planes, ROWS, nz)
    sizes = step_sizes(SWEEPS)
    depth = SWEEPS
    bits = members.bit_length() - 1
    f32 = jnp.float32

    swap = [(m, m ^ 1) for m in range(members)]

    def pair(step):
        order = [list(range(1, bits)), list(range(2, bits)) + [1]]
        return [(m, m ^ (1 << order[m % 2][step])) for m in range(members)]

    def along(mine):
        moves = []
        for m in range(members):
            step = -1 if (m % 2 == 0) == mine else 1
            for s in range(subs):
                moves.append((m * subs + s, m * subs + (s + step) % subs))
        return moves

    other = lax.ppermute(velocity, "member", swap)
    vp, gp, first, last = call(
        arrange_kernel,
        [(comps, nx, *layer)] * 2 + [(comps, 1, *layer)] * 2,
        [velocity, forcing],
        10 * velocity.size,
        name="arrange",
    )
    above = lax.ppermute(first, "sub", [(s, (s - 1) % subs) for s in range(subs)])
    below = lax.ppermute(last, "sub", [(s, (s + 1) % subs) for s in range(subs)])
    hold = []
    if FAKE:
        hold = call(gate_kernel, [(FAKE, 1, *layer)], [below, above], 1, name="gate")
        hold = [lax.ppermute(hold[0], "member", swap)]
    parts = list(call(
        functools.partial(sums_kernel, PIECES),
        [(comps + 1, far - near, *layer) for near, far in PIECES],
        [vp, other],
        6 * velocity.size,
        name="sums",
    ))
    got = [None] * len(parts)
    for step in range(bits - 1):
        for i, part in enumerate(parts):
            if step:
                tie = [parts[i - 1]] if i else []
                if i and step == 1:
                    tie += hold or [below, above]
                parts[i] = part = call(
                    add_kernel, [part.shape], [part, got[i]] + tie, part.size, name="add%d" % i
                )[0]
            got[i] = lax.ppermute(part, "member", pair(step))
    stats_mine, stats_theirs, src_mine, src_theirs, halo_mine, halo_theirs = [], [], [], [], [], []
    tie = parts[1:]
    for i, ((near, far), part, last_got) in enumerate(zip(PIECES, parts, got)):
        terms = [part] if last_got is None else [part, last_got]
        stats = call(
            functools.partial(stats_kernel, members, len(terms) == 2),
            [(comps - 1, far - near, *layer), (2, far - near, *layer)],
            terms + tie,
            10 * part.size,
            name="stats%d" % i,
        )
        swapped = [lax.ppermute(x, "member", swap) for x in stats]
        stats_mine.append(stats[1])
        stats_theirs.append(swapped[1])
        mine, theirs = call(
            functools.partial(source_kernel, (near, far)),
            [(comps, far - near, *layer)] * 2,
            [vp, gp, below, above, *stats, *swapped],
            20 * part.size,
            name="source%d" % i,
        )
        mines, theirses = [mine], [theirs]
        src_mine.append(mine)
        src_theirs.append(theirs)
        for mine_part, theirs_part in zip(mines, theirses):
            halo_mine.append(lax.ppermute(mine_part, ("member", "sub"), along(True)))
            halo_theirs.append(lax.ppermute(theirs_part, ("member", "sub"), along(False)))
        tie = [mine]
    visc = call(pick_kernel, [stats_mine[0].shape[1:]], stats_mine, 1, name="pick")[0]
    visc_mine = lax.ppermute(visc, ("member", "sub"), along(True))

    own = call(
        functools.partial(own_kernel, PIECES, sizes, nx),
        [(2, 7, depth, *layer), (2, comps, depth, *layer), (depth, 2, comps, 2, *layer), (2, depth, *layer)],
        src_mine + src_theirs + stats_mine + stats_theirs,
        20 * 3 * velocity.size,
        scratch=[pltpu.VMEM((depth, 2, comps, depth, *layer), f32)],
        name="own",
    )
    coef_own, scaled_own, edges, visc_own = own
    visc_mine, padded = call(
        share_kernel,
        [visc.shape, (PAD + visc.shape[0], *layer)],
        [visc_mine, halo_mine[0], halo_theirs[0], edges],
        1,
        name="share",
    )
    visc_halo = [visc_mine] + [
        lax.ppermute(value, "member", [(m, m ^ hop) for m in range(members)])
        for hop, value in ((1, padded), (2, visc_mine), (3, visc_mine))
    ]
    olds, scaled_old, parts = [], [], []
    for n, (piece, mine, theirs) in enumerate(zip(STAGES, halo_mine, halo_theirs)):
        first, final = n == 0, n == len(STAGES) - 1
        width = piece[1] - piece[0]
        ins = [coef_own]
        ins += [visc_own, *visc_halo] if first else [coef_halo]
        ins += [scaled_own] + scaled_old + [edges, mine, theirs]
        scratch = [pltpu.VMEM((depth, 2, comps, width + 2, *layer), f32)]
        if first:
            scratch.append(pltpu.VMEM((2, depth + 2, *layer), f32))
        if final:
            ins += parts
            outs = [velocity.shape]
            scratch += [
                pltpu.VMEM((2, comps, width, *layer), f32),
                pltpu.VMEM((2, comps, width, ny, nz), f32),
                pltpu.SemaphoreType.DMA((2 * len(STAGES),)),
            ]
        else:
            outs = [
                (2, comps, width + 1, *layer),
                (depth, 2, comps, 2, *layer),
                (2, comps, width, ny, nz),
            ]
            if first:
                outs.append((2, 7, depth + 1, *layer))
        results = call(
            functools.partial(stage_kernel, PIECES, piece, first, final, sizes, nx, list(olds)),
            outs,
            ins,
            20 * width * velocity.size,
            scratch=scratch,
            any_out=final,
            name="stage%d" % n,
        )
        if final:
            return results[0]
        if first:
            coef_halo = results[3]
        olds.append(piece)
        scaled_old.append(results[0])
        edges = results[1]
        parts.append(results[2])


def solution(mesh):
    in_specs = (P("member", None, "sub", None, None), P("member", None, "sub", None, None))
    out_specs = P("member", None, "sub", None, None)
    return jax.shard_map(fast, mesh=mesh, in_specs=in_specs, out_specs=out_specs, check_vma=False)
```

```python
import functools
import math

import jax
import jax.numpy as jnp
from jax import lax
from jax.experimental import pallas as pl
from jax.experimental.pallas import tpu as pltpu
from jax.sharding import PartitionSpec as P

SWEEPS = 8


TIME_STEP = 0.25
EDDY_COEFF = 1.0
BASE_VISCOSITY = 1.0
LOWER_EDGE = 0.1
UPPER_EDGE = 1.9

ROWS = 8
PIECES = ((0, 4), (4, 8))
STAGES = ((0, 4), (4, 8))
PAD = 5
FAKE = 9
VMEM_LIMIT = 40 * 1024 * 1024


def step_sizes(sweep_count):
    middle = (UPPER_EDGE + LOWER_EDGE) / 2
    radius = (UPPER_EDGE - LOWER_EDGE) / 2
    return [
        1.0 / (middle + radius * math.cos(math.pi * (2 * position + 1) / (2 * sweep_count)))
        for position in range(sweep_count)
    ]


def north(planes, j):
    return planes[j + 1] if j + 1 < len(planes) else pltpu.roll(planes[0], ROWS - 1, 0)


def south(planes, j):
    return planes[j - 1] if j else pltpu.roll(planes[-1], 1, 0)


def upper(plane):
    return pltpu.roll(plane, plane.shape[-1] - 1, 1)


def lower(plane):
    return pltpu.roll(plane, 1, 1)


def rows_of(j, count):
    return pl.ds(j, ROWS, stride=count)


def parity():
    return lax.rem(lax.axis_index("member"), 2)


def for_layers(count, body, unroll=1):
    def step(i, carry):
        body(i)
        return carry

    lax.fori_loop(0, count, step, 0, unroll=unroll)


def arrange_kernel(vel, vp, first, last):
    comps, nx, planes = vp.shape[:3]

    def body(x):
        for c in range(comps):
            for j in range(planes):
                vp[c, x, j] = vel[0, c, x, rows_of(j, planes), :]

    for_layers(nx, body, 2)
    first[...] = vp[:, :1]
    last[...] = vp[:, nx - 1 :]


def push_kernel(vp, force, gp):
    comps, nx, planes = vp.shape[:3]

    def body(x):
        for c in range(comps):
            for j in range(planes):
                gp[c, x, j] = vp[c, x, j] + TIME_STEP * force[0, c, x, rows_of(j, planes), :]

    for_layers(nx, body, 2)


def sums_kernel(pieces, vp, other, *refs):
    outs = refs[len(refs) - len(pieces) :]
    comps, nx, planes = vp.shape[:3]
    side = parity()
    for (near, far), out in zip(pieces, outs):
        start = jnp.where(side == 0, near, nx - far)

        def body(i, out=out, start=start):
            x = start + i
            for j in range(planes):
                squares = None
                for c in range(comps):
                    a = vp[c, x, j]
                    b = other[0, c, x, rows_of(j, planes), :]
                    out[c, i, j] = a + b
                    both = a * a + b * b
                    squares = both if squares is None else squares + both
                out[comps, i, j] = squares

        for_layers(far - near, body)


def add_kernel(*refs):
    refs[-1][...] = refs[0][...] + refs[1][...]


def quarter():
    return lax.rem(lax.axis_index("member") // 2, 2)


def gate_kernel(*refs):
    count = refs[0].shape[0]
    refs[-1][:count] = refs[0][...]


def share_kernel(*refs):
    count = refs[0].shape[0]
    refs[-2][...] = refs[0][...]
    refs[-1][:count] = refs[0][...]


def pick_kernel(first, second, out):
    out[...] = jnp.where(quarter() == 0, first[1], second[1])


def stats_kernel(members, add_two, *refs):
    flow, rest = refs[-2:]
    comps, layers, planes = refs[0].shape[0] - 1, refs[0].shape[1], refs[0].shape[2]

    def body(i):
        for j in range(planes):
            def total(c):
                value = refs[0][c, i, j]
                return value + refs[1][c, i, j] if add_two else value

            spread = total(comps) * (1.0 / members)
            for c in range(comps):
                mean = total(c) * (1.0 / members)
                if c < comps - 1:
                    flow[c, i, j] = mean
                else:
                    rest[0, i, j] = mean
                spread = spread - mean * mean
            rest[1, i, j] = BASE_VISCOSITY + EDDY_COEFF * TIME_STEP * spread

    for_layers(layers, body)


def source_kernel(piece, vp, gp, below, above, mine, mine_rest, theirs, theirs_rest, *refs):
    out_mine, out_theirs = refs[-2:]
    comps, nx, planes = vp.shape[:3]
    near, far = piece
    side = parity()
    for which, stats, rest, out in (
        (side, mine, mine_rest, out_mine),
        (1 - side, theirs, theirs_rest, out_theirs),
    ):
        start = jnp.where(which == 0, near, nx - far)

        def body(i, stats=stats, rest=rest, out=out, start=start):
            x = start + i
            down, up = jnp.maximum(x - 1, 0), jnp.minimum(x + 1, nx - 1)
            for c in range(comps):
                here = [vp[c, x, j] for j in range(planes)]
                for j in range(planes):
                    west = jnp.where(x == 0, below[c, 0, j], vp[c, down, j])
                    east = jnp.where(x == nx - 1, above[c, 0, j], vp[c, up, j])
                    transport = (
                        stats[0, i, j] * (east - west)
                        + stats[1, i, j] * (north(here, j) - south(here, j))
                        + rest[0, i, j] * (upper(here[j]) - lower(here[j]))
                    )
                    out[c, i, j] = gp[c, x, j] - (0.5 * TIME_STEP) * transport

        for_layers(far - near, body, far - near)


def relaxed(center, outward, inward, coef, source, comps, planes, step_size):
    here = [[center(c, j) for j in range(planes)] for c in range(comps)]
    values = []
    for j in range(planes):
        faces = [coef(a, j) for a in range(6)]
        for c in range(comps):
            ns, ss = north(here[c], j), south(here[c], j)
            image = source(c, j) + faces[0] * inward(c, j)
            image = image + faces[1] * outward(c, j)
            image = image + (faces[2] * ns + faces[3] * ss)
            image = image + (faces[4] * upper(here[c][j]) + faces[5] * lower(here[c][j]))
            values.append((c, j, (1.0 - step_size) * here[c][j] + step_size * image))
    return values


class Taker:
    def __init__(self, refs):
        self.refs, self.at = refs, 0

    def __call__(self, n=1):
        self.at += n
        return list(self.refs[self.at - n : self.at])


def make_coefs(visc_here, visc_in, visc_out, put, planes):
    half = 0.5 * TIME_STEP
    for j in range(planes):
        here = visc_here[j]
        faces = [
            here + visc_in[j],
            here + visc_out[j],
            here + north(visc_here, j),
            here + south(visc_here, j),
            here + upper(here),
            here + lower(here),
        ]
        total = (faces[0] + faces[1]) + (faces[2] + faces[3]) + (faces[4] + faces[5])
        inverse = 1.0 / (1.0 + half * total)
        scale = half * inverse
        for a in range(6):
            put(a, j, faces[a] * scale)
        put(6, j, inverse)


def run_sweeps(reach, before, sizes, comps, planes, load, coef, source, keep, last):
    depth = len(sizes)
    for k in range(1, depth + 1):
        layers = range(k + depth - reach, min(k + depth - before, 2 * depth))
        for s in range(2):
            found = []
            for i in layers:
                found.append(
                    relaxed(
                        lambda c, j: load(k - 1, s, c, i, j),
                        lambda c, j: load(k - 1, s, c, i - 1, j),
                        lambda c, j: load(k - 1, s, c, i + 1, j),
                        lambda a, j: coef(s, a, i, j),
                        lambda c, j: source(s, c, i, j),
                        comps,
                        planes,
                        sizes[k - 1],
                    )
                )
            for i, values in zip(layers, found):
                for c, j, value in values:
                    if k < depth:
                        keep(k, s, c, i, j, value)
                    else:
                        last(s, c, i, j, value)


def own_kernel(pieces, sizes, count, *refs):
    number = len(pieces)
    take = Taker(refs)
    src_mine, src_theirs = take(number), take(number)
    stat_mine, stat_theirs = take(number), take(number)
    coef, scaled, edges, visc = take(4)
    (field,) = take(1)
    depth = len(sizes)
    comps, planes = scaled.shape[1], scaled.shape[3]
    side = parity()
    for which, stats, srcs in ((side, stat_mine, src_mine), (1 - side, stat_theirs, src_theirs)):
        for (near, far), stat, src in zip(pieces, stats, srcs):
            for e in range(far - near):
                d = jnp.where(which == 0, near + e, far - 1 - e)
                visc[which, d] = stat[1, e]
                for c in range(comps):
                    field[0, which, c, d] = src[c, e]
    for s in range(2):
        for d in range(1, depth):
            def put(a, j, value):
                coef[s, a, d, j] = value

            make_coefs(
                [visc[s, d, j] for j in range(planes)],
                [visc[s, d + 1, j] if d + 1 < depth else visc[1 - s, d, j] for j in range(planes)],
                [visc[s, d - 1, j] for j in range(planes)],
                put,
                planes,
            )
            for c in range(comps):
                for j in range(planes):
                    scaled[s, c, d, j] = field[0, s, c, d, j] * coef[s, 6, d, j]

    def load(k, s, c, i, j):
        return field[k, s, c, i - depth, j] if i < 2 * depth else field[k, 1 - s, c, depth - 1, j]

    def keep(k, s, c, i, j, value):
        field[k, s, c, i - depth, j] = value

    triangle(sizes, comps, planes, load, coef, scaled, keep)
    for k in range(depth):
        for s in range(2):
            for c in range(comps):
                edges[k, s, c, 0] = field[k, s, c, k]
                edges[k, s, c, 1] = (
                    field[k, s, c, k + 1] if k + 1 < depth else field[k, 1 - s, c, depth - 1]
                )


def triangle(sizes, comps, planes, load, coef, scaled, keep):
    depth = len(sizes)
    for k in range(1, depth):
        for s in range(2):
            layers = range(k + depth, 2 * depth)
            found = [
                relaxed(
                    lambda c, j: load(k - 1, s, c, i, j),
                    lambda c, j: load(k - 1, s, c, i - 1, j),
                    lambda c, j: load(k - 1, s, c, i + 1, j),
                    lambda a, j: coef[s, a, i - depth, j],
                    lambda c, j: scaled[s, c, i - depth, j],
                    comps,
                    planes,
                    sizes[k - 1],
                )
                for i in layers
            ]
            for i, values in zip(layers, found):
                for c, j, value in values:
                    keep(k, s, c, i, j, value)


def stage_kernel(pieces, piece, first, final, sizes, count, olds, *refs):
    take = Taker(refs)
    depth = len(sizes)
    near, far = piece
    width = far - near
    (coef_own,) = take()
    if first:
        (visc_own,) = take()
        visc_halo = take(4)
    else:
        (coef_halo,) = take()
    scaled_own = take()[0]
    scaled_old = take(len(olds))
    edges_in, halo_mine, halo_theirs = take(3)
    if final:
        parts = take(len(olds))
        (out,) = take()
    else:
        scaled_new, edges, part = take(3)
        if first:
            (coef_halo,) = take()
    (field,) = take()
    if first:
        (visc,) = take()
    if final:
        scaled_new, tail, sems = take(3)
    comps, planes = scaled_own.shape[1], scaled_own.shape[3]
    side = parity()

    copies = []
    if final:
        for n, ((lo, hi), done) in enumerate(zip(olds, parts)):
            for s in range(2):
                where = depth - hi if s == 0 else count - depth + lo
                copies.append(
                    pltpu.make_async_copy(
                        done.at[s], out.at[0, :, where : where + hi - lo], sems.at[2 * n + s]
                    )
                )
                copies[-1].start()

    for which, halo in ((side, halo_mine), (1 - side, halo_theirs)):
        for e in range(width):
            spot = jnp.where(which == 0, width - 1 - e, e)
            for c in range(comps):
                field[0, 1 - which, c, spot] = halo[c, e]
    for k in range(depth):
        for s in range(2):
            for c in range(comps):
                for e in range(2):
                    field[k, s, c, width + e] = edges_in[k, s, c, e]

    if first:
        length = pieces[0][1] - pieces[0][0]
        for hop, got in enumerate(visc_halo):
            which = side if hop % 2 == 0 else 1 - side
            lo = length * (quarter() if hop < 2 else 1 - quarter())
            for e in range(length):
                i = jnp.where(which == 0, depth - 1 - lo - e, depth - lo - length + e)
                visc[1 - which, i] = got[e]
        for s in range(2):
            for d in range(2):
                visc[s, depth + d] = visc_own[s, d]
        for s in range(2):
            for i in range(1, depth + 1):
                def put(a, j, value):
                    coef_halo[s, a, i, j] = value

                make_coefs(
                    [visc[s, i, j] for j in range(planes)],
                    [visc[s, i + 1, j] for j in range(planes)],
                    [visc[s, i - 1, j] for j in range(planes)],
                    put,
                    planes,
                )

    def coef(s, a, i, j):
        return coef_halo[s, a, i, j] if i <= depth else coef_own[s, a, i - depth, j]

    base = depth - far
    for s in range(2):
        for p in range(width):
            i = base + p
            if i > 0:
                for c in range(comps):
                    for j in range(planes):
                        scaled_new[s, c, p, j] = field[0, s, c, p, j] * coef_halo[s, 6, i, j]
        if first:
            for c in range(comps):
                for j in range(planes):
                    scaled_new[s, c, width, j] = edges_in[0, s, c, 0, j] * coef_halo[s, 6, depth, j]

    def source(s, c, i, j):
        if i > depth:
            return scaled_own[s, c, i - depth, j]
        if first:
            return scaled_new[s, c, i - base, j]
        if i == depth:
            lo, hi = olds[0]
            return scaled_old[0][s, c, hi - lo, j]
        d = depth - 1 - i
        if near <= d < far:
            return scaled_new[s, c, i - base, j]
        for (lo, hi), ref in zip(olds, scaled_old):
            if lo <= d < hi:
                return ref[s, c, i - (depth - hi), j]
        raise ValueError("no source")

    def load(k, s, c, i, j):
        return field[k, s, c, i - (k + depth - far), j]

    def keep(k, s, c, i, j, value):
        field[k, s, c, i - (k + depth - far), j] = value

    def last(s, c, i, j, value):
        p = i - (2 * depth - far)
        place = p if s == 0 else width - 1 - p
        target = tail if final else part
        target[s, c, place, rows_of(j, planes), :] = value

    run_sweeps(far, near, sizes, comps, planes, load, coef, source, keep, last)

    if final:
        for s in range(2):
            where = depth - far if s == 0 else count - depth + near
            copies.append(
                pltpu.make_async_copy(
                    tail.at[s], out.at[0, :, where : where + width], sems.at[2 * len(olds) + s]
                )
            )
            copies[-1].start()
        for copy in copies:
            copy.wait()
    else:
        for k in range(depth):
            for s in range(2):
                for c in range(comps):
                    for e in range(2):
                        edges[k, s, c, e] = field[k, s, c, e]


def vmem(n):
    return [pl.BlockSpec(memory_space=pltpu.VMEM)] * n


def call(kernel, outs, ins, flops, scratch=(), any_out=False, name=None):
    shapes = [jax.ShapeDtypeStruct(shape, jnp.float32) for shape in outs]
    size = 4 * sum(math.prod(shape) for shape in outs) + 4 * sum(x.size for x in ins)
    result = pl.pallas_call(
        kernel,
        out_shape=shapes,
        in_specs=vmem(len(ins)),
        out_specs=[pl.BlockSpec(memory_space=pl.ANY)] * len(outs) if any_out else vmem(len(outs)),
        scratch_shapes=list(scratch),
        compiler_params=pltpu.CompilerParams(vmem_limit_bytes=VMEM_LIMIT),
        cost_estimate=pl.CostEstimate(flops=flops, bytes_accessed=size, transcendentals=0),
        name=name,
    )(*ins)
    return result


def fast(velocity, forcing):
    members = lax.axis_size("member")
    subs = lax.axis_size("sub")
    _, comps, nx, ny, nz = velocity.shape
    planes = ny // ROWS
    layer = (planes, ROWS, nz)
    sizes = step_sizes(SWEEPS)
    depth = SWEEPS
    bits = members.bit_length() - 1
    f32 = jnp.float32

    swap = [(m, m ^ 1) for m in range(members)]

    def pair(step):
        order = [list(range(1, bits)), list(range(2, bits)) + [1]]
        return [(m, m ^ (1 << order[m % 2][step])) for m in range(members)]

    def along(mine):
        moves = []
        for m in range(members):
            step = -1 if (m % 2 == 0) == mine else 1
            for s in range(subs):
                moves.append((m * subs + s, m * subs + (s + step) % subs))
        return moves

    other = lax.ppermute(velocity, "member", swap)
    vp, first, last = call(
        arrange_kernel,
        [(comps, nx, *layer)] + [(comps, 1, *layer)] * 2,
        [velocity],
        velocity.size,
        name="arrange",
    )
    gp = call(push_kernel, [vp.shape], [vp, forcing], 2 * velocity.size, name="push")[0]
    above = lax.ppermute(first, "sub", [(s, (s - 1) % subs) for s in range(subs)])
    below = lax.ppermute(last, "sub", [(s, (s + 1) % subs) for s in range(subs)])
    hold = []
    if FAKE:
        hold = call(gate_kernel, [(FAKE, 1, *layer)], [below, above], 1, name="gate")
        hold = [lax.ppermute(hold[0], "member", swap)]
    parts = list(call(
        functools.partial(sums_kernel, PIECES),
        [(comps + 1, far - near, *layer) for near, far in PIECES],
        [vp, other],
        6 * velocity.size,
        name="sums",
    ))
    got = [None] * len(parts)
    for step in range(bits - 1):
        for i, part in enumerate(parts):
            if step:
                tie = [parts[i - 1]] if i else []
                if i and step == 1:
                    tie += (hold or [below, above]) + [gp]
                parts[i] = part = call(
                    add_kernel, [part.shape], [part, got[i]] + tie, part.size, name="add%d" % i
                )[0]
            got[i] = lax.ppermute(part, "member", pair(step))
    stats_mine, stats_theirs, src_mine, src_theirs, halo_mine, halo_theirs = [], [], [], [], [], []
    tie = parts[1:]
    for i, ((near, far), part, last_got) in enumerate(zip(PIECES, parts, got)):
        terms = [part] if last_got is None else [part, last_got]
        stats = call(
            functools.partial(stats_kernel, members, len(terms) == 2),
            [(comps - 1, far - near, *layer), (2, far - near, *layer)],
            terms + tie,
            10 * part.size,
            name="stats%d" % i,
        )
        swapped = [lax.ppermute(x, "member", swap) for x in stats]
        stats_mine.append(stats[1])
        stats_theirs.append(swapped[1])
        mine, theirs = call(
            functools.partial(source_kernel, (near, far)),
            [(comps, far - near, *layer)] * 2,
            [vp, gp, below, above, *stats, *swapped],
            20 * part.size,
            name="source%d" % i,
        )
        mines, theirses = [mine], [theirs]
        src_mine.append(mine)
        src_theirs.append(theirs)
        for mine_part, theirs_part in zip(mines, theirses):
            halo_mine.append(lax.ppermute(mine_part, ("member", "sub"), along(True)))
            halo_theirs.append(lax.ppermute(theirs_part, ("member", "sub"), along(False)))
        tie = [mine]
    visc = call(pick_kernel, [stats_mine[0].shape[1:]], stats_mine, 1, name="pick")[0]
    visc_mine = lax.ppermute(visc, ("member", "sub"), along(True))

    own = call(
        functools.partial(own_kernel, PIECES, sizes, nx),
        [(2, 7, depth, *layer), (2, comps, depth, *layer), (depth, 2, comps, 2, *layer), (2, depth, *layer)],
        src_mine + src_theirs + stats_mine + stats_theirs,
        20 * 3 * velocity.size,
        scratch=[pltpu.VMEM((depth, 2, comps, depth, *layer), f32)],
        name="own",
    )
    coef_own, scaled_own, edges, visc_own = own
    visc_mine, padded = call(
        share_kernel,
        [visc.shape, (PAD + visc.shape[0], *layer)],
        [visc_mine, halo_mine[0], halo_theirs[0], edges],
        1,
        name="share",
    )
    visc_halo = [visc_mine] + [
        lax.ppermute(value, "member", [(m, m ^ hop) for m in range(members)])
        for hop, value in ((1, padded), (2, visc_mine), (3, visc_mine))
    ]
    olds, scaled_old, parts = [], [], []
    for n, (piece, mine, theirs) in enumerate(zip(STAGES, halo_mine, halo_theirs)):
        first, final = n == 0, n == len(STAGES) - 1
        width = piece[1] - piece[0]
        ins = [coef_own]
        ins += [visc_own, *visc_halo] if first else [coef_halo]
        ins += [scaled_own] + scaled_old + [edges, mine, theirs]
        scratch = [pltpu.VMEM((depth, 2, comps, width + 2, *layer), f32)]
        if first:
            scratch.append(pltpu.VMEM((2, depth + 2, *layer), f32))
        if final:
            ins += parts
            outs = [velocity.shape]
            scratch += [
                pltpu.VMEM((2, comps, width, *layer), f32),
                pltpu.VMEM((2, comps, width, ny, nz), f32),
                pltpu.SemaphoreType.DMA((2 * len(STAGES),)),
            ]
        else:
            outs = [
                (2, comps, width + 1, *layer),
                (depth, 2, comps, 2, *layer),
                (2, comps, width, ny, nz),
            ]
            if first:
                outs.append((2, 7, depth + 1, *layer))
        results = call(
            functools.partial(stage_kernel, PIECES, piece, first, final, sizes, nx, list(olds)),
            outs,
            ins,
            20 * width * velocity.size,
            scratch=scratch,
            any_out=final,
            name="stage%d" % n,
        )
        if final:
            return results[0]
        if first:
            coef_halo = results[3]
        olds.append(piece)
        scaled_old.append(results[0])
        edges = results[1]
        parts.append(results[2])


def solution(mesh):
    in_specs = (P("member", None, "sub", None, None), P("member", None, "sub", None, None))
    out_specs = P("member", None, "sub", None, None)
    return jax.shard_map(fast, mesh=mesh, in_specs=in_specs, out_specs=out_specs, check_vma=False)
```
